128 devices in a mesh: dp: 4 (over x), expert: 32 (over z, y, core).
Axes of the slice: x: 4, y: 4, z: 4, core: 2. Of those that a mesh axis runs over, the one named last changes fastest.
Arguments:
- tokens: bfloat16 [32768, 2048], P(('dp', 'expert')), may hold values from -6 to 6
- out_grad: bfloat16 [32768, 2048], P(('dp', 'expert')), may hold values from -6 to 6
- picks: int32 [4, 32, 128], P('dp', 'expert'), may hold values from 0 to 8191, as said below
- gates: float32 [4, 32, 128], P('dp', 'expert'), may hold values from 0.1 to 1
- w_in: bfloat16 [32, 2048, 4096], P('expert', None, 'dp'), may hold values from -0.125 to 0.125
- w_out: bfloat16 [32, 4096, 2048], P('expert', 'dp'), may hold values from -0.09375 to 0.09375
Outputs:
- moe_out: bfloat16 [32768, 2048], P(('dp', 'expert'))
- tokens_grad: bfloat16 [32768, 2048], P(('dp', 'expert'))
- w_in_grad: bfloat16 [32, 2048, 4096], P('expert', None, 'dp')
- w_out_grad: bfloat16 [32, 4096, 2048], P('expert', 'dp')
The draws below stay inside these ranges and needn't reach their ends.
Inputs may be any that keep to these rules, and one draw needn't show every extreme that they name: Indices of tokens within one group; the 128 picks of one expert in one group are distinct; among the tokens of one device (an aligned block of 256) an expert picks at most 8, and this is reached in every draw.
All inputs are finite; a program needn't handle non-finite values.
Results may differ from the reference program's by a relative error of at most 0.015.
Values may be sent and summed in bfloat16 or wider, within the bound.
No kernel may reach another device: no remote copies, remote signals or barrier semaphores. Data moves between devices by JAX's collectives and lax.ppermute only.
A program may use at most 128 MiB of HBM per device.

```python
import math
import jax
import jax.numpy as jnp
from jax import lax

D = 2048
FF = 4096
TOK_DEV = 256
EXPERTS = 32
CAP = 128
SLOT = 8
TOKENS = 32768
N_DP = 4
N_EXPERT = 32


def draw_picks(key, part):
    key = jax.random.fold_in(key, 7)
    key_counts, key_places, key_order = jax.random.split(key, 3)
    quarter = N_EXPERT // 4
    pattern = jnp.concatenate([jnp.full((quarter,), SLOT, jnp.int32), jnp.full((quarter,), SLOT // 2, jnp.int32), jnp.full((quarter,), 3 * SLOT // 8, jnp.int32), jnp.full((quarter,), SLOT // 8, jnp.int32)])
    list_count = N_DP * EXPERTS

    def permute_pattern(one_key):
        return jax.random.permutation(one_key, pattern)

    def first_places(one_key):
        return jax.random.permutation(one_key, TOK_DEV)[:SLOT].astype(jnp.int32)

    def permute_picks(one_key):
        return jax.random.permutation(one_key, CAP).astype(jnp.int32)
    counts = jax.vmap(permute_pattern)(jax.random.split(key_counts, list_count))
    places = jax.vmap(first_places)(jax.random.split(key_places, list_count * N_EXPERT))
    places = places.reshape(list_count, N_EXPERT, SLOT)
    blocks = jnp.arange(N_EXPERT, dtype=jnp.int32)[None, :, None] * TOK_DEV
    candidates = (blocks + places).reshape(list_count, N_EXPERT * SLOT)
    is_valid = (jnp.arange(SLOT, dtype=jnp.int32)[None, None, :] < counts[:, :, None]).reshape(list_count, N_EXPERT * SLOT)
    ordering = jnp.argsort(1 - is_valid.astype(jnp.int32), axis=1, stable=True)[:, :CAP]
    chosen = jnp.take_along_axis(candidates, ordering, axis=1)
    shuffles = jax.vmap(permute_picks)(jax.random.split(key_order, list_count))
    chosen = jnp.take_along_axis(chosen, shuffles, axis=1)
    return chosen.reshape(N_DP, EXPERTS, CAP).astype(jnp.int32)


def steps_of(own_key, extent, shards, low, high):
    level, own = 1.0, jax.random.fold_in(own_key, 6)
    for dim, parts in shards:
        heights = jnp.exp(jax.random.uniform(jax.random.fold_in(own, dim), (parts,), jnp.float32, low / len(shards), high / len(shards)))
        level = level * jnp.repeat(heights, extent[dim] // parts).reshape([-1 if axis == dim else 1 for axis in range(len(extent))])
    return level


def normal_values(own_key, dims, spread, bound, pieces=(), held_as=jnp.bfloat16):
    array = jax.random.normal(own_key, dims, jnp.float32) * spread
    if len(pieces) > 0:
        array = steps_of(own_key, dims, pieces, -0.22, 0.18) * array
    return jnp.clip(array, min=-bound, max=bound).astype(held_as)


def setup_inputs(seed: int = 0) -> dict:
    streams_of = jax.random.split(jax.random.key(seed), 7)
    tokens = normal_values(streams_of[0], (TOKENS, D), 1.0, 6.0, ((0, 128),))
    out_grad = normal_values(streams_of[1], (TOKENS, D), 1.0, 6.0, ((0, 128),))
    picks = draw_picks(jax.random.fold_in(streams_of[6], 71), 0)
    gates = jnp.clip(jnp.exp(math.log(1.0) - 2.3025851 * jax.random.uniform(streams_of[3], (N_DP, EXPERTS, CAP), jnp.float32) ** steps_of(streams_of[3], (N_DP, EXPERTS, CAP), ((0, 4), (1, 32)), -0.2, 0.2)), 0.1, 1.0)
    w_in = normal_values(streams_of[4], (EXPERTS, D, FF), D ** -0.5, 0.125, ((0, 32), (2, 4)))
    w_out = normal_values(streams_of[5], (EXPERTS, FF, D), FF ** -0.5, 0.09375, ((0, 32), (1, 4)))
    return {"tokens": tokens, "out_grad": out_grad, "picks": picks, "gates": gates, "w_in": w_in, "w_out": w_out}


def rounded(values):
    return lax.optimization_barrier(values.astype(jnp.bfloat16)).astype(jnp.float32)

def reference(tokens, out_grad, picks, gates, w_in, w_out):
    offsets = jnp.arange(N_DP, dtype=jnp.int32) * (TOK_DEV * N_EXPERT)
    quarter = FF // N_DP

    def per_expert(expert):
        row_ids = (picks[:, expert, :] + offsets[:, None]).reshape(-1).astype(jnp.int32)
        inputs = tokens[row_ids]
        cotangents = out_grad[row_ids]
        gate_rows = gates[:, expert, :].reshape(-1)
        weight_in = w_in[expert]
        weight_out = w_out[expert]
        act = jnp.dot(inputs, weight_in, preferred_element_type=jnp.float32)
        hidden, gelu_back = jax.vjp(jax.nn.gelu, act)
        hidden = hidden.astype(jnp.bfloat16)
        hid_parts = hidden.reshape(-1, N_DP, quarter).astype(jnp.float32)
        out_parts = weight_out.reshape(N_DP, quarter, D).astype(jnp.float32)
        summed = lax.optimization_barrier(jnp.sum(rounded(jnp.einsum('rsk,skd->srd', hid_parts, out_parts)), axis=0))
        outputs = (gate_rows[:, None] * summed).astype(jnp.bfloat16)
        dout = (gate_rows[:, None] * cotangents.astype(jnp.float32)).astype(jnp.bfloat16)
        dhid = lax.dot_general(dout, weight_out, (((1,), (1,)), ((), ())), preferred_element_type=jnp.float32)
        dact = gelu_back(dhid)[0].astype(jnp.bfloat16)
        dact_parts = dact.reshape(-1, N_DP, quarter).astype(jnp.float32)
        in_parts = weight_in.reshape(D, N_DP, quarter).astype(jnp.float32)
        dinput = lax.optimization_barrier(jnp.sum(rounded(jnp.einsum('rsk,dsk->srd', dact_parts, in_parts)), axis=0)).astype(jnp.bfloat16)
        grad_in = lax.dot_general(inputs, dact, (((0,), (0,)), ((), ())), preferred_element_type=jnp.float32).astype(jnp.bfloat16)
        grad_out = lax.dot_general(hidden, dout, (((0,), (0,)), ((), ())), preferred_element_type=jnp.float32).astype(jnp.bfloat16)
        return (outputs, dinput, grad_in, grad_out)
    outs_all, dins_all, grads_in, grads_out = lax.map(per_expert, jnp.arange(EXPERTS, dtype=jnp.int32))
    all_rows = jnp.transpose(picks + offsets[:, None, None], (1, 0, 2)).reshape(-1).astype(jnp.int32)
    zero_rows = jnp.zeros((TOKENS, D), jnp.float32)
    moe_out = zero_rows.at[all_rows].add(outs_all.reshape(-1, D).astype(jnp.float32)).astype(jnp.bfloat16)
    tokens_grad = zero_rows.at[all_rows].add(dins_all.reshape(-1, D).astype(jnp.float32)).astype(jnp.bfloat16)
    return (moe_out, tokens_grad, grads_in, grads_out)
```

```python
import jax
import jax.numpy as jnp
from jax import lax
from jax.sharding import PartitionSpec as P

F32 = jnp.float32
BF16 = jnp.bfloat16


def shifted(array, step):
    count = lax.axis_size("dp")
    return lax.ppermute(array, "dp", [(i, (i + step) % count) for i in range(count)])


def ring_gather(own):
    half = own.shape[0] // 2
    below = shifted(own, 1)
    above = shifted(own, -1)
    far_upper = shifted(below[:half], 1)
    far_lower = shifted(above[half:], -1)
    return own, below, above, far_upper, far_lower


def ring_sum(parts):
    own, below, above, far = jnp.split(parts, 4, axis=0)
    half = own.shape[0] // 2
    far = far.astype(BF16)
    to_above = shifted(far[:half], 1)
    to_below = shifted(far[half:], -1)
    above = jnp.concatenate(
        [(above[:half] + to_above.astype(F32)).astype(BF16), above[half:].astype(BF16)], axis=0
    )
    below = jnp.concatenate(
        [below[:half].astype(BF16), (below[half:] + to_below.astype(F32)).astype(BF16)], axis=0
    )
    from_below = shifted(above, 1)
    from_above = shifted(below, -1)
    return own + from_below.astype(F32) + from_above.astype(F32)


def swap(array):
    return lax.all_to_all(array, "expert", split_axis=0, concat_axis=0, tiled=True)


def on_device(tokens, out_grad, picks, gates, w_in, w_out):
    experts = lax.axis_size("expert")
    tok_dev, width = tokens.shape
    capacity = picks.shape[2]
    slot_size = 2 * capacity // experts
    slots = experts * slot_size

    own_picks = picks[0, 0]
    source = own_picks // tok_dev
    order = jnp.arange(capacity, dtype=jnp.int32)
    earlier = (source[None, :] == source[:, None]) & (order[None, :] < order[:, None])
    rank = jnp.sum(earlier.astype(jnp.int32), axis=1)
    slot_of = source * slot_size + rank
    place = slot_of[None, :] == jnp.arange(slots, dtype=jnp.int32)[:, None]
    wanted = jnp.sum(jnp.where(place, own_picks[None, :] % tok_dev + 1, 0), axis=1)
    wanted = jnp.broadcast_to(wanted.astype(F32)[:, None], (slots, 128))
    place = place.astype(BF16)

    asked = swap(wanted.reshape(experts, slot_size, 128)).reshape(slots, 128)[:, :1]
    layout = (
        asked.astype(jnp.int32) == jnp.arange(1, tok_dev + 1, dtype=jnp.int32)[None, :]
    ).astype(BF16)

    def send(rows):
        packed = jnp.dot(layout, rows, preferred_element_type=F32).astype(BF16)
        return swap(packed.reshape(experts, slot_size, width)).reshape(slots, width)

    def unslot(rows):
        return lax.dot_general(place, rows, (((0,), (0,)), ((), ())), preferred_element_type=F32)

    def back(rows):
        placed = jnp.dot(place, rows, preferred_element_type=F32).astype(BF16)
        came = swap(placed.reshape(experts, slot_size, width)).reshape(slots, width)
        return lax.dot_general(
            layout, came, (((0,), (0,)), ((), ())), preferred_element_type=F32
        ).astype(BF16)

    own_gates = gates[0, 0][:, None]
    weight_in = w_in[0]
    weight_out = w_out[0]

    came_in = send(tokens)
    came_in, out_grad = lax.optimization_barrier((came_in, out_grad))
    came_cot = send(out_grad)
    inputs = ring_gather(unslot(came_in).astype(BF16))
    dout_own = (own_gates * unslot(came_cot)).astype(BF16)
    dout_own, inputs = lax.optimization_barrier((dout_own, inputs))
    dout = ring_gather(dout_own)
    inputs = jnp.concatenate(inputs, axis=0)
    dout = jnp.concatenate(dout, axis=0)

    act = jnp.dot(inputs, weight_in, preferred_element_type=F32)
    hidden, gelu_back = jax.vjp(jax.nn.gelu, act)
    hidden = hidden.astype(BF16)
    part = jnp.dot(hidden, weight_out, preferred_element_type=F32)
    summed = ring_sum(part)
    outputs = (own_gates * summed).astype(BF16)

    dhid = lax.dot_general(dout, weight_out, (((1,), (1,)), ((), ())), preferred_element_type=F32)
    dact = gelu_back(dhid)[0].astype(BF16)
    dpart = lax.dot_general(dact, weight_in, (((1,), (1,)), ((), ())), preferred_element_type=F32)
    outputs, dpart = lax.optimization_barrier((outputs, dpart))
    moe_out = back(outputs)
    dinput = ring_sum(dpart).astype(BF16)
    tokens_grad = back(dinput)

    grad_in = lax.dot_general(
        inputs, dact, (((0,), (0,)), ((), ())), preferred_element_type=F32
    ).astype(BF16)
    grad_out = lax.dot_general(
        hidden, dout, (((0,), (0,)), ((), ())), preferred_element_type=F32
    ).astype(BF16)
    return (moe_out, tokens_grad, grad_in[None], grad_out[None])


def solution(mesh):
    return jax.shard_map(
        on_device,
        mesh=mesh,
        in_specs=(
            P(("dp", "expert"), None),
            P(("dp", "expert"), None),
            P("dp", "expert", None),
            P("dp", "expert", None),
            P("expert", None, "dp"),
            P("expert", "dp", None),
        ),
        out_specs=(
            P(("dp", "expert"), None),
            P(("dp", "expert"), None),
            P("expert", None, "dp"),
            P("expert", "dp", None),
        ),
        check_vma=False,
    )
```

```python
import functools

import jax
import jax.numpy as jnp
from jax import lax
from jax.experimental import pallas as pl
from jax.experimental.pallas import tpu as pltpu
from jax.sharding import PartitionSpec as P

F32 = jnp.float32
BF16 = jnp.bfloat16


def shifted(array, step):
    count = lax.axis_size("dp")
    return lax.ppermute(array, "dp", [(i, (i + step) % count) for i in range(count)])


def ring_gather(own):
    half = own.shape[0] // 2
    below = shifted(own, 1)
    above = shifted(own, -1)
    far_upper = shifted(below[:half], 1)
    far_lower = shifted(above[half:], -1)
    return own, below, above, far_upper, far_lower


def ring_sum(parts):
    own, below, above, far = jnp.split(parts, 4, axis=0)
    half = own.shape[0] // 2
    far = far.astype(BF16)
    to_above = shifted(far[:half], 1)
    to_below = shifted(far[half:], -1)
    above = jnp.concatenate(
        [(above[:half] + to_above.astype(F32)).astype(BF16), above[half:].astype(BF16)], axis=0
    )
    below = jnp.concatenate(
        [below[:half].astype(BF16), (below[half:] + to_below.astype(F32)).astype(BF16)], axis=0
    )
    from_below = shifted(above, 1)
    from_above = shifted(below, -1)
    return own + from_below.astype(F32) + from_above.astype(F32)


def swap(array):
    return lax.all_to_all(array, "expert", split_axis=0, concat_axis=0, tiled=True)


def ask_kernel(tok_dev, slot_size, picks, wanted):
    capacity, slots = picks.shape[1], wanted.shape[0]
    own = picks[...]
    source = own // tok_dev
    square = (capacity, capacity)
    down = lax.broadcasted_iota(jnp.int32, square, 0)
    across = lax.broadcasted_iota(jnp.int32, square, 1)
    turned = jnp.sum(jnp.where(down == across, source, 0), axis=1, keepdims=True)
    earlier = (turned == source) & (down < across)
    rank = jnp.sum(earlier.astype(jnp.int32), axis=0, keepdims=True)
    slot = lax.broadcasted_iota(jnp.int32, (slots, capacity), 0)
    here = slot == source * slot_size + rank
    token = jnp.sum(jnp.where(here, own - source * tok_dev + 1, 0), axis=1, keepdims=True)
    wanted[...] = jnp.broadcast_to(token.astype(F32), wanted.shape)


def on_device(tokens, out_grad, picks, gates, w_in, w_out):
    experts = lax.axis_size("expert")
    tok_dev, width = tokens.shape
    capacity = picks.shape[2]
    slot_size = 2 * capacity // experts
    slots = experts * slot_size

    own_picks = picks[0, 0]
    source = own_picks // tok_dev
    order = jnp.arange(capacity, dtype=jnp.int32)
    earlier = (source[None, :] == source[:, None]) & (order[None, :] < order[:, None])
    rank = jnp.sum(earlier.astype(jnp.int32), axis=1)
    slot_of = source * slot_size + rank
    place = slot_of[None, :] == jnp.arange(slots, dtype=jnp.int32)[:, None]
    wanted = pl.pallas_call(
        functools.partial(ask_kernel, tok_dev, slot_size),
        out_shape=jax.ShapeDtypeStruct((slots, 128), F32),
        compiler_params=pltpu.CompilerParams(vmem_limit_bytes=4 * 2**20),
    )(picks[0])
    place = place.astype(BF16)

    asked = swap(wanted.reshape(experts, slot_size, 128)).reshape(slots, 128)[:, :1]
    layout = (
        asked.astype(jnp.int32) == jnp.arange(1, tok_dev + 1, dtype=jnp.int32)[None, :]
    ).astype(BF16)

    def pack(rows):
        packed = jnp.dot(layout, rows, preferred_element_type=F32).astype(BF16)
        return packed.reshape(experts, slot_size, width)

    def unslot(rows):
        return lax.dot_general(place, rows, (((0,), (0,)), ((), ())), preferred_element_type=F32)

    def back(rows):
        placed = jnp.dot(place, rows, preferred_element_type=F32).astype(BF16)
        came = swap(placed.reshape(experts, slot_size, width)).reshape(slots, width)
        return lax.dot_general(
            layout, came, (((0,), (0,)), ((), ())), preferred_element_type=F32
        ).astype(BF16)

    own_gates = gates[0, 0][:, None]
    weight_in = w_in[0]
    weight_out = w_out[0]

    came_in = swap(pack(tokens)).reshape(slots, width)
    packed_cot, came_in = lax.optimization_barrier((pack(out_grad), came_in))
    came_cot = swap(packed_cot).reshape(slots, width)
    inputs = ring_gather(unslot(came_in).astype(BF16))
    inputs = jnp.concatenate(inputs, axis=0)
    came_cot, inputs = lax.optimization_barrier((came_cot, inputs))
    dout_own = (own_gates * unslot(came_cot)).astype(BF16)
    dout_own, inputs = lax.optimization_barrier((dout_own, inputs))
    dout = ring_gather(dout_own)

    act = jnp.dot(inputs, weight_in, preferred_element_type=F32)
    hidden, gelu_back = jax.vjp(jax.nn.gelu, act)
    hidden = hidden.astype(BF16)
    part = jnp.dot(hidden, weight_out, preferred_element_type=F32)
    part, *near = lax.optimization_barrier((part, *dout[:3]))
    dout = jnp.concatenate([*near, *dout[3:]], axis=0)
    summed = ring_sum(part)
    outputs = (own_gates * summed).astype(BF16)

    dhid = lax.dot_general(dout, weight_out, (((1,), (1,)), ((), ())), preferred_element_type=F32)
    dact = gelu_back(dhid)[0].astype(BF16)
    dpart = lax.dot_general(dact, weight_in, (((1,), (1,)), ((), ())), preferred_element_type=F32)
    outputs, dpart = lax.optimization_barrier((outputs, dpart))
    moe_out = back(outputs)
    dinput = ring_sum(dpart).astype(BF16)
    tokens_grad = back(dinput)

    grad_in = lax.dot_general(
        inputs, dact, (((0,), (0,)), ((), ())), preferred_element_type=F32
    ).astype(BF16)
    grad_out = lax.dot_general(
        hidden, dout, (((0,), (0,)), ((), ())), preferred_element_type=F32
    ).astype(BF16)
    return (moe_out, tokens_grad, grad_in[None], grad_out[None])


def solution(mesh):
    return jax.shard_map(
        on_device,
        mesh=mesh,
        in_specs=(
            P(("dp", "expert"), None),
            P(("dp", "expert"), None),
            P("dp", "expert", None),
            P("dp", "expert", None),
            P("expert", None, "dp"),
            P("expert", "dp", None),
        ),
        out_specs=(
            P(("dp", "expert"), None),
            P(("dp", "expert"), None),
            P("expert", None, "dp"),
            P("expert", "dp", None),
        ),
        check_vma=False,
    )
```

```python
import functools

import jax
import jax.numpy as jnp
from jax import lax
from jax.experimental import pallas as pl
from jax.experimental.pallas import tpu as pltpu
from jax.sharding import PartitionSpec as P

F32 = jnp.float32
BF16 = jnp.bfloat16


def shifted(array, step):
    count = lax.axis_size("dp")
    return lax.ppermute(array, "dp", [(i, (i + step) % count) for i in range(count)])


def ring_gather(own):
    half = own.shape[0] // 2
    below = shifted(own, 1)
    above = shifted(own, -1)
    far_upper = shifted(below[:half], 1)
    far_lower = shifted(above[half:], -1)
    return own, below, above, far_upper, far_lower


def ring_sum(parts):
    own, below, above, far = jnp.split(parts, 4, axis=0)
    half = own.shape[0] // 2
    far = far.astype(BF16)
    to_above = shifted(far[:half], 1)
    to_below = shifted(far[half:], -1)
    above = jnp.concatenate(
        [(above[:half] + to_above.astype(F32)).astype(BF16), above[half:].astype(BF16)], axis=0
    )
    below = jnp.concatenate(
        [below[:half].astype(BF16), (below[half:] + to_below.astype(F32)).astype(BF16)], axis=0
    )
    from_below = shifted(above, 1)
    from_above = shifted(below, -1)
    return own + from_below.astype(F32) + from_above.astype(F32)


def added(first, second):
    return first.astype(F32) + second.astype(F32)


def joined_sum(parts):
    own, below, above, far = jnp.split(parts, 4, axis=0)
    half = own.shape[0] // 2
    up = shifted(jnp.concatenate([far[:half], above[half:]], axis=0), 1)
    down = shifted(jnp.concatenate([far[half:], below[:half]], axis=0), -1)
    merged_upper = added(above[:half], up[:half]).astype(BF16)
    merged_lower = added(below[half:], down[:half]).astype(BF16)
    merged_upper, merged_lower = lax.optimization_barrier((merged_upper, merged_lower))
    merged_upper = shifted(merged_upper, 1)
    merged_lower = shifted(merged_lower, -1)
    upper = added(own[:half], down[half:]) + merged_upper.astype(F32)
    lower = added(own[half:], up[half:]) + merged_lower.astype(F32)
    return jnp.concatenate([upper, lower], axis=0)


def swap(array):
    return lax.all_to_all(array, "expert", split_axis=0, concat_axis=0, tiled=True)


def ask_kernel(tok_dev, slot_size, picks, wanted):
    capacity, slots = picks.shape[1], wanted.shape[0]
    own = picks[...]
    source = own // tok_dev
    square = (capacity, capacity)
    down = lax.broadcasted_iota(jnp.int32, square, 0)
    across = lax.broadcasted_iota(jnp.int32, square, 1)
    turned = jnp.sum(jnp.where(down == across, source, 0), axis=1, keepdims=True)
    earlier = (turned == source) & (down < across)
    rank = jnp.sum(earlier.astype(jnp.int32), axis=0, keepdims=True)
    slot = lax.broadcasted_iota(jnp.int32, (slots, capacity), 0)
    here = slot == source * slot_size + rank
    token = jnp.sum(jnp.where(here, own - source * tok_dev + 1, 0), axis=1, keepdims=True)
    wanted[...] = jnp.broadcast_to(token.astype(F32), wanted.shape)


def on_device(tokens, out_grad, picks, gates, w_in, w_out):
    experts = lax.axis_size("expert")
    tok_dev, width = tokens.shape
    capacity = picks.shape[2]
    slot_size = 2 * capacity // experts
    slots = experts * slot_size

    own_picks = picks[0, 0]
    source = own_picks // tok_dev
    order = jnp.arange(capacity, dtype=jnp.int32)
    earlier = (source[None, :] == source[:, None]) & (order[None, :] < order[:, None])
    rank = jnp.sum(earlier.astype(jnp.int32), axis=1)
    slot_of = source * slot_size + rank
    place = slot_of[None, :] == jnp.arange(slots, dtype=jnp.int32)[:, None]
    wanted = pl.pallas_call(
        functools.partial(ask_kernel, tok_dev, slot_size),
        out_shape=jax.ShapeDtypeStruct((slots, 128), F32),
        compiler_params=pltpu.CompilerParams(vmem_limit_bytes=4 * 2**20),
    )(picks[0])
    place = place.astype(BF16)

    asked = swap(wanted.reshape(experts, slot_size, 128)).reshape(slots, 128)[:, :1]
    layout = (
        asked.astype(jnp.int32) == jnp.arange(1, tok_dev + 1, dtype=jnp.int32)[None, :]
    ).astype(BF16)

    def pack(rows):
        packed = jnp.dot(layout, rows, preferred_element_type=F32).astype(BF16)
        return packed.reshape(experts, slot_size, width)

    def unslot(rows):
        return lax.dot_general(place, rows, (((0,), (0,)), ((), ())), preferred_element_type=F32)

    def put(rows):
        return jnp.dot(place, rows, preferred_element_type=F32).astype(BF16)

    def back(placed):
        came = swap(placed.reshape(experts, slot_size, width)).reshape(slots, width)
        return lax.dot_general(
            layout, came, (((0,), (0,)), ((), ())), preferred_element_type=F32
        ).astype(BF16)

    own_gates = gates[0, 0][:, None]
    weight_in = w_in[0]
    weight_out = w_out[0]

    came_in = swap(pack(tokens)).reshape(slots, width)
    packed_cot, came_in = lax.optimization_barrier((pack(out_grad), came_in))
    came_cot = swap(packed_cot).reshape(slots, width)
    inputs = ring_gather(unslot(came_in).astype(BF16))
    inputs = list(inputs)
    inputs[:2] = lax.optimization_barrier((inputs[0], inputs[1]))
    inputs = jnp.concatenate(inputs, axis=0)
    came_cot, inputs = lax.optimization_barrier((came_cot, inputs))
    dout_own = (own_gates * unslot(came_cot)).astype(BF16)
    dout_own, inputs = lax.optimization_barrier((dout_own, inputs))
    dout = ring_gather(dout_own)

    act = jnp.dot(inputs, weight_in, preferred_element_type=F32)
    hidden, gelu_back = jax.vjp(jax.nn.gelu, act)
    hidden = hidden.astype(BF16)
    part = jnp.dot(hidden, weight_out, preferred_element_type=F32)
    part, *near = lax.optimization_barrier((part, *dout[:3]))
    dout = jnp.concatenate([*near, *dout[3:]], axis=0)
    summed = ring_sum(part)
    outputs = (own_gates * summed).astype(BF16)

    dhid = lax.dot_general(dout, weight_out, (((1,), (1,)), ((), ())), preferred_element_type=F32)
    dact = gelu_back(dhid)[0].astype(BF16)
    dpart = lax.dot_general(
        dact, weight_in, (((1,), (1,)), ((), ())), preferred_element_type=F32
    ).astype(BF16)
    placed, dpart = lax.optimization_barrier((put(outputs), dpart))
    moe_out = back(placed)
    dinput = joined_sum(dpart).astype(BF16)
    tokens_grad = back(put(dinput))

    grad_in = lax.dot_general(
        inputs, dact, (((0,), (0,)), ((), ())), preferred_element_type=F32
    ).astype(BF16)
    grad_out = lax.dot_general(
        hidden, dout, (((0,), (0,)), ((), ())), preferred_element_type=F32
    ).astype(BF16)
    return (moe_out, tokens_grad, grad_in[None], grad_out[None])


def solution(mesh):
    return jax.shard_map(
        on_device,
        mesh=mesh,
        in_specs=(
            P(("dp", "expert"), None),
            P(("dp", "expert"), None),
            P("dp", "expert", None),
            P("dp", "expert", None),
            P("expert", None, "dp"),
            P("expert", "dp", None),
        ),
        out_specs=(
            P(("dp", "expert"), None),
            P(("dp", "expert"), None),
            P("expert", None, "dp"),
            P("expert", "dp", None),
        ),
        check_vma=False,
    )
```

```python
import functools

import jax
import jax.numpy as jnp
from jax import lax
from jax.experimental import pallas as pl
from jax.experimental.pallas import tpu as pltpu
from jax.sharding import PartitionSpec as P

F32 = jnp.float32
BF16 = jnp.bfloat16


def shifted(array, step):
    count = lax.axis_size("dp")
    return lax.ppermute(array, "dp", [(i, (i + step) % count) for i in range(count)])


def ring_gather(own):
    half = own.shape[0] // 2
    below = shifted(own, 1)
    above = shifted(own, -1)
    far_upper = shifted(below[:half], 1)
    far_lower = shifted(above[half:], -1)
    return own, below, above, far_upper, far_lower


def ring_sum(parts):
    own, below, above, far = jnp.split(parts, 4, axis=0)
    half = own.shape[0] // 2
    far = far.astype(BF16)
    to_above = shifted(far[:half], 1)
    to_below = shifted(far[half:], -1)
    above = jnp.concatenate(
        [(above[:half] + to_above.astype(F32)).astype(BF16), above[half:].astype(BF16)], axis=0
    )
    below = jnp.concatenate(
        [below[:half].astype(BF16), (below[half:] + to_below.astype(F32)).astype(BF16)], axis=0
    )
    above, below = lax.optimization_barrier((above, below))
    from_below = shifted(above, 1)
    from_above = shifted(below, -1)
    return own + from_below.astype(F32) + from_above.astype(F32)


def added(first, second):
    return first.astype(F32) + second.astype(F32)


def joined_sum(parts):
    own, below, above, far = jnp.split(parts, 4, axis=0)
    half = own.shape[0] // 2
    up = shifted(jnp.concatenate([far[:half], above[half:]], axis=0), 1)
    down = shifted(jnp.concatenate([far[half:], below[:half]], axis=0), -1)
    merged_upper = added(above[:half], up[:half]).astype(BF16)
    merged_lower = added(below[half:], down[:half]).astype(BF16)
    merged_upper, merged_lower = lax.optimization_barrier((merged_upper, merged_lower))
    merged_upper = shifted(merged_upper, 1)
    merged_lower = shifted(merged_lower, -1)
    upper = added(own[:half], down[half:]) + merged_upper.astype(F32)
    lower = added(own[half:], up[half:]) + merged_lower.astype(F32)
    return jnp.concatenate([upper, lower], axis=0)


def swap(array):
    return lax.all_to_all(array, "expert", split_axis=0, concat_axis=0, tiled=True)


def ask_kernel(tok_dev, slot_size, picks, wanted):
    capacity, slots = picks.shape[1], wanted.shape[0]
    own = picks[...]
    source = own // tok_dev
    square = (capacity, capacity)
    down = lax.broadcasted_iota(jnp.int32, square, 0)
    across = lax.broadcasted_iota(jnp.int32, square, 1)
    turned = jnp.sum(jnp.where(down == across, source, 0), axis=1, keepdims=True)
    earlier = (turned == source) & (down < across)
    rank = jnp.sum(earlier.astype(jnp.int32), axis=0, keepdims=True)
    slot = lax.broadcasted_iota(jnp.int32, (slots, capacity), 0)
    here = slot == source * slot_size + rank
    token = jnp.sum(jnp.where(here, own - source * tok_dev + 1, 0), axis=1, keepdims=True)
    wanted[...] = jnp.broadcast_to(token.astype(F32), wanted.shape)


def on_device(tokens, out_grad, picks, gates, w_in, w_out):
    experts = lax.axis_size("expert")
    tok_dev, width = tokens.shape
    capacity = picks.shape[2]
    slot_size = 2 * capacity // experts
    slots = experts * slot_size

    own_picks = picks[0, 0]
    source = own_picks // tok_dev
    order = jnp.arange(capacity, dtype=jnp.int32)
    earlier = (source[None, :] == source[:, None]) & (order[None, :] < order[:, None])
    rank = jnp.sum(earlier.astype(jnp.int32), axis=1)
    slot_of = source * slot_size + rank
    place = slot_of[None, :] == jnp.arange(slots, dtype=jnp.int32)[:, None]
    wanted = pl.pallas_call(
        functools.partial(ask_kernel, tok_dev, slot_size),
        out_shape=jax.ShapeDtypeStruct((slots, 128), F32),
        compiler_params=pltpu.CompilerParams(vmem_limit_bytes=4 * 2**20),
    )(picks[0])
    place = place.astype(BF16)

    asked = swap(wanted.reshape(experts, slot_size, 128)).reshape(slots, 128)[:, :1]
    layout = (
        asked.astype(jnp.int32) == jnp.arange(1, tok_dev + 1, dtype=jnp.int32)[None, :]
    ).astype(BF16)

    def pack(rows):
        packed = jnp.dot(layout, rows, preferred_element_type=F32).astype(BF16)
        return packed.reshape(experts, slot_size, width)

    def unslot(rows):
        return lax.dot_general(place, rows, (((0,), (0,)), ((), ())), preferred_element_type=F32)

    def put(rows):
        return jnp.dot(place, rows, preferred_element_type=F32).astype(BF16)

    def back(placed):
        came = swap(placed.reshape(experts, slot_size, width)).reshape(slots, width)
        return lax.dot_general(
            layout, came, (((0,), (0,)), ((), ())), preferred_element_type=F32
        ).astype(BF16)

    own_gates = gates[0, 0][:, None]
    weight_in = w_in[0]
    weight_out = w_out[0]

    came_in = swap(pack(tokens)).reshape(slots, width)
    packed_cot, came_in = lax.optimization_barrier((pack(out_grad), came_in))
    came_cot = swap(packed_cot).reshape(slots, width)
    inputs = ring_gather(unslot(came_in).astype(BF16))
    inputs = list(inputs)
    inputs[:2] = lax.optimization_barrier((inputs[0], inputs[1]))
    inputs = jnp.concatenate(inputs, axis=0)
    came_cot, inputs = lax.optimization_barrier((came_cot, inputs))
    dout_own = (own_gates * unslot(came_cot)).astype(BF16)
    dout_own, inputs = lax.optimization_barrier((dout_own, inputs))
    dout = ring_gather(dout_own)

    act = jnp.dot(inputs, weight_in, preferred_element_type=F32)
    hidden, gelu_back = jax.vjp(jax.nn.gelu, act)
    hidden = hidden.astype(BF16)
    part = jnp.dot(hidden, weight_out, preferred_element_type=F32)
    part, *near = lax.optimization_barrier((part, *dout[:3]))
    dout = jnp.concatenate([*near, *dout[3:]], axis=0)
    summed = ring_sum(part)
    outputs = (own_gates * summed).astype(BF16)

    dhid = lax.dot_general(dout, weight_out, (((1,), (1,)), ((), ())), preferred_element_type=F32)
    dact = gelu_back(dhid)[0].astype(BF16)
    dpart = lax.dot_general(
        dact, weight_in, (((1,), (1,)), ((), ())), preferred_element_type=F32
    ).astype(BF16)
    placed, dpart = lax.optimization_barrier((put(outputs), dpart))
    moe_out = back(placed)
    dinput = joined_sum(dpart).astype(BF16)
    tokens_grad = back(put(dinput))

    grad_in = lax.dot_general(
        inputs, dact, (((0,), (0,)), ((), ())), preferred_element_type=F32
    ).astype(BF16)
    grad_out = lax.dot_general(
        hidden, dout, (((0,), (0,)), ((), ())), preferred_element_type=F32
    ).astype(BF16)
    return (moe_out, tokens_grad, grad_in[None], grad_out[None])


def solution(mesh):
    return jax.shard_map(
        on_device,
        mesh=mesh,
        in_specs=(
            P(("dp", "expert"), None),
            P(("dp", "expert"), None),
            P("dp", "expert", None),
            P("dp", "expert", None),
            P("expert", None, "dp"),
            P("expert", "dp", None),
        ),
        out_specs=(
            P(("dp", "expert"), None),
            P(("dp", "expert"), None),
            P("expert", None, "dp"),
            P("expert", "dp", None),
        ),
        check_vma=False,
    )
```
